32 devices in a mesh: groups: 1, date: 32 (over z, y, x, core), tile: 1, pol: 1.
Axes of the slice: x: 2, y: 2, z: 4, core: 2. Of those that a mesh axis runs over, the one named last changes fastest.
Arguments:
- slc: bfloat16 [2, 256, 16, 128], P(None, ('date', 'pol'), ('groups', 'tile')), as said below
- date_group: int32 [32], replicated, may hold values from 0 to 31, each once
- ref_blocks: int32 [16], replicated, may hold values from 0 to 15, each once
- look_offsets: int32 [4], replicated, may hold values from 0 to 3, each once
Outputs:
- coherence: float32 [2, 4, 32, 64, 256], P(None, ('groups', 'tile', 'pol'), 'date')
The draws below stay inside these ranges and needn't reach their ends.
Inputs may be any that keep to these rules, and one draw needn't show every extreme that they name: `date_group`: a permutation; storage rows s*8 + k hold date date_group[s]*8 + k. `ref_blocks`: a permutation of the date blocks. `look_offsets`: a permutation. `slc`: every pixel's amplitude sqrt(re^2 + im^2) lies between 0.49 and 2.02.
All inputs are finite; a program needn't handle non-finite values.
Results may differ from the reference program's by a relative error of at most 0.0003.
Values may be sent and summed in bfloat16 or wider, within the bound.
A program may use at most 64 MiB of HBM per device.

```python
import math
import jax
import jax.numpy as jnp
from jax import lax

DATES = 256
REF_BLK = 16
NREF = 4
STRIDE = 4
WIN = 9
STORE_GROUPS = 32
ROWS = 16
COLS = 128
LR = 4
LC = 32


def draw_slc(key, part):
    keys = jax.random.split(key, 4)
    shape = (DATES, ROWS, COLS)
    amplitude = jnp.exp(jax.random.uniform(keys[0], shape, jnp.float32, math.log(0.5), math.log(2.0)))
    spread = jnp.exp(jax.random.uniform(keys[1], (DATES, 1, 1), jnp.float32, math.log(0.15), math.log(3.0)))
    common = jax.random.uniform(keys[2], (1, ROWS, COLS), jnp.float32, -math.pi, math.pi)
    jitter = jax.random.normal(keys[3], shape, jnp.float32)
    phase = common + spread * jitter
    return jnp.stack([amplitude * jnp.cos(phase), amplitude * jnp.sin(phase)]).astype(jnp.bfloat16)


def setup_inputs(seed: int = 0, part: int = 0) -> dict:
    key_of = jax.random.split(jax.random.key(seed), 5)
    part_splits = jax.random.split(jax.random.fold_in(key_of[4], part), 5)
    slc = draw_slc(jax.random.fold_in(jax.random.fold_in(key_of[4], part), 71), part)
    date_group = jax.random.permutation(key_of[1], STORE_GROUPS).astype(jnp.int32)
    ref_blocks = jax.random.permutation(key_of[2], DATES // REF_BLK).astype(jnp.int32)
    look_offsets = jax.random.permutation(key_of[3], STRIDE).astype(jnp.int32)
    return dict(slc=slc, date_group=date_group, ref_blocks=ref_blocks, look_offsets=look_offsets)


def box_matrix(look_count, cell_count, grid_offset, cell_shift):
    look_ids = jnp.arange(look_count, dtype=jnp.int32)[:, None]
    cell_ids = jnp.arange(cell_count, dtype=jnp.int32)[None, :]
    distance = jnp.abs(cell_ids - cell_shift - STRIDE * look_ids - grid_offset)
    return (distance <= WIN // 2).astype(jnp.float32)

def windowed(surface, row_box, col_box):
    across = jnp.einsum('...qw,cw->...qc', surface, col_box, precision=lax.Precision.HIGHEST)
    return jnp.einsum('aq,...qc->...ac', row_box, across, precision=lax.Precision.HIGHEST)

def slot_order(date_group, dates_here):
    block_count = date_group.shape[0]
    block_ids = jnp.arange(block_count, dtype=jnp.int32)
    matches = (date_group[None, :] == block_ids[:, None]).astype(jnp.int32)
    inverse = lax.optimization_barrier(jnp.sum(matches * block_ids[None, :], axis=1))
    date_slots = inverse[:, None] * dates_here + jnp.arange(dates_here, dtype=jnp.int32)[None, :]
    return (inverse, date_slots.reshape(-1))

def pair_terms(real_one, imag_one, real_many, imag_many):
    return jnp.stack([real_one * real_many + imag_one * imag_many, imag_one * real_many - real_one * imag_many])

def reference(slc, date_group, ref_blocks, look_offsets):
    dates_here = DATES // date_group.shape[0]
    inverse, date_slots = slot_order(date_group, dates_here)
    by_date = jnp.take(slc, date_slots, axis=1).astype(jnp.float32)
    ref_index = (ref_blocks[:NREF, None] * REF_BLK + jnp.arange(REF_BLK, dtype=jnp.int32)[None, :]).reshape(-1)
    ref_vals = jnp.take(by_date, ref_index, axis=1)
    row_box = box_matrix(LR, ROWS, look_offsets[0], 0)
    col_box = box_matrix(LC, COLS, look_offsets[1], 0)
    date_power = windowed(by_date[0] * by_date[0] + by_date[1] * by_date[1], row_box, col_box)
    ref_power = jnp.take(date_power, ref_index, axis=0)

    def one_date(entries):
        real_one, imag_one, own_power = entries
        numerator = windowed(pair_terms(real_one[None], imag_one[None], ref_vals[0], ref_vals[1]), row_box, col_box)
        return numerator / jnp.sqrt(own_power[None, None] * ref_power[None])
    coherence = lax.map(one_date, (by_date[0], by_date[1], date_power))
    return jnp.transpose(coherence, (1, 3, 4, 2, 0))
```

```python
import functools

import jax
import jax.numpy as jnp
from jax import lax
from jax.experimental import pallas as pl
from jax.experimental.pallas import tpu as pltpu
from jax.sharding import PartitionSpec as P

REF_BLK = 16
NREF = 4
STRIDE = 4
WIN = 9
RIM = WIN // 2
SPAN = 3


def with_halo(cells, axis, dim, width):
    count = lax.axis_size(axis)
    ends = count - 1
    head = lax.slice_in_dim(cells, 0, width, axis=dim)
    tail = lax.slice_in_dim(cells, cells.shape[dim] - width, cells.shape[dim], axis=dim)
    return jnp.concatenate(
        [
            lax.ppermute(tail, axis, [(i, i + 1) for i in range(ends)]),
            cells,
            lax.ppermute(head, axis, [(i + 1, i) for i in range(ends)]),
        ],
        axis=dim,
    )


def nt_dot(a, b):
    return lax.dot_general(
        a, b, (((1,), (1,)), ((), ())), preferred_element_type=jnp.float32
    )


def iota(shape, dim):
    return lax.broadcasted_iota(jnp.int32, shape, dim)


def pack(x_ref, p, col_blocks):
    _, _, days, rows, cols = x_ref.shape
    lanes = 2 * rows * STRIDE
    tall = jnp.concatenate(
        [jnp.concatenate([x_ref[p, 0, d], x_ref[p, 1, d]], axis=0) for d in range(days)], axis=1
    )
    spread = (iota((lanes, 2 * rows), 0) // STRIDE == iota((lanes, 2 * rows), 1))
    wide = jnp.dot(spread.astype(jnp.bfloat16), tall, preferred_element_type=jnp.float32)
    keep = iota(wide.shape, 0) % STRIDE == iota(wide.shape, 1) % STRIDE
    wide = jnp.where(keep, wide, 0.0).astype(jnp.bfloat16)
    shape = (col_blocks * days, days * cols)
    row_id, lane_id = iota(shape, 0), iota(shape, 1)
    pick = (row_id // days == (lane_id % cols) // STRIDE) & (row_id % days == lane_id // cols)
    pick = jnp.where(pick, 1.0, 0.0).astype(jnp.bfloat16)
    return nt_dot(pick, wide).reshape(col_blocks, days, lanes)


def exchange_kernel(n_date, n_pol, x_ref, got_ref, blocks, send_sem, recv_sem):
    n = n_date * n_pol
    my_date, my_pol = lax.axis_index("date"), lax.axis_index("pol")
    me = my_date * n_pol + my_pol

    def place(k):
        other = lax.rem(me + k, n)
        return other // n_pol, lax.rem(other, n_pol)

    barrier = pltpu.get_barrier_semaphore()

    def greet(k, carry):
        date, pol = place(k)
        pl.semaphore_signal(
            barrier,
            inc=1,
            device_id={"date": date, "pol": pol},
            device_id_type=pl.DeviceIdType.MESH,
        )
        return carry

    lax.fori_loop(1, n, greet, 0)

    zero = jnp.zeros((1,) + blocks.shape[2:], blocks.dtype)
    for p in range(n_pol):
        blocks[p, 0:1] = zero
        blocks[p, n_date + 1 : n_date + 2] = zero
        blocks[p, 1 : n_date + 1] = pack(x_ref, p, n_date).astype(blocks.dtype)

    pl.semaphore_wait(barrier, n - 1)

    def send(k, carry):
        date, pol = place(k)
        pltpu.make_async_remote_copy(
            src_ref=blocks.at[pol, pl.ds(date, SPAN)],
            dst_ref=got_ref.at[me],
            send_sem=send_sem,
            recv_sem=recv_sem,
            device_id={"date": date, "pol": pol},
            device_id_type=pl.DeviceIdType.MESH,
        ).start()
        return carry

    lax.fori_loop(1, n, send, 0)
    pltpu.make_async_copy(
        blocks.at[my_pol, pl.ds(my_date, SPAN)], got_ref.at[me], recv_sem
    ).start()
    pltpu.make_async_copy(got_ref, got_ref, recv_sem).wait()
    sent = got_ref.at[pl.ds(0, n - 1)]
    pltpu.make_async_copy(sent, sent, send_sem).wait()


def exchange(x, n_date, n_pol):
    _, _, days, rows, _ = x.shape
    lanes = 2 * rows * STRIDE
    n = n_date * n_pol
    return pl.pallas_call(
        functools.partial(exchange_kernel, n_date, n_pol),
        out_shape=jax.ShapeDtypeStruct((n, SPAN, days, lanes), x.dtype),
        in_specs=[pl.BlockSpec(memory_space=pltpu.VMEM)],
        out_specs=pl.BlockSpec(memory_space=pltpu.VMEM),
        scratch_shapes=[
            pltpu.VMEM((n_pol, n_date + SPAN - 1, days, lanes), x.dtype),
            pltpu.SemaphoreType.DMA,
            pltpu.SemaphoreType.DMA,
        ],
        compiler_params=pltpu.CompilerParams(
            collective_id=0, has_side_effects=True, vmem_limit_bytes=24 * 1024 * 1024
        ),
    )(x)


def look_kernel(days, row_base, group_ref, refs_ref, offs_ref, got_ref, out_ref):
    sources = group_ref.shape[0]
    dates = sources * days
    if got_ref.shape[0] == SPAN:
        stored = [got_ref[m] for m in range(SPAN)]
    else:
        stored = [
            got_ref[:, m].astype(jnp.float32).reshape(dates, got_ref.shape[-1]).astype(jnp.bfloat16)
            for m in range(SPAN)
        ]
    lanes = stored[0].shape[1]
    stored = jnp.concatenate(stored, axis=1)
    width = SPAN * lanes

    slot = iota((1, dates), 1)
    held = jnp.zeros((1, dates), jnp.int32)
    for s in range(sources):
        held = jnp.where(slot // days == s, group_ref[s], held)
    held = held * days + slot % days
    ref_id = iota((NREF * REF_BLK, 1), 0)
    wanted = jnp.zeros(ref_id.shape, jnp.int32)
    for b in range(NREF):
        wanted = jnp.where(ref_id // REF_BLK == b, refs_ref[b], wanted)
    wanted = wanted * REF_BLK + ref_id % REF_BLK
    order = jnp.where(iota((dates, dates), 0) == held, 1.0, 0.0).astype(jnp.bfloat16)
    ref_order = jnp.where(wanted == held, 1.0, 0.0).astype(jnp.bfloat16)
    vals = jnp.dot(order, stored, preferred_element_type=jnp.float32)
    refs = jnp.dot(ref_order, stored, preferred_element_type=jnp.float32)

    half = lanes // 2
    turned = jnp.concatenate(
        [pltpu.roll(refs[:, m * lanes : (m + 1) * lanes], half, 1) for m in range(SPAN)], axis=1
    )
    turned = jnp.where(iota(turned.shape, 1) % lanes < half, -turned, turned)

    def window(rows, look):
        lane = iota((rows, width), 1)
        col = (lane // lanes - 1) * STRIDE + lane % STRIDE - offs_ref[1]
        row = (lane % half) // STRIDE + row_base - STRIDE * look - offs_ref[0]
        return (jnp.abs(col) <= RIM) & (jnp.abs(row) <= RIM)

    looks = out_ref.shape[1]
    square = vals * vals
    high = square.astype(jnp.bfloat16)
    low = (square - high.astype(jnp.float32)).astype(jnp.bfloat16)
    boxes = jnp.where(window(8, iota((8, width), 0)), 1.0, 0.0).astype(jnp.bfloat16)
    scale = lax.rsqrt(nt_dot(boxes, high) + nt_dot(boxes, low))

    parts, ref_scale = [], []
    for i in range(looks):
        box = jnp.where(window(1, i), 1.0, 0.0)
        here = refs * box
        parts += [here.astype(jnp.bfloat16), (turned * box).astype(jnp.bfloat16)]
        ref_scale.append(lax.rsqrt(jnp.sum(here * here, axis=1, keepdims=True)))
    num = nt_dot(jnp.concatenate(parts, axis=0), vals.astype(jnp.bfloat16))
    count = NREF * REF_BLK
    for i in range(looks):
        both = scale[i : i + 1] * ref_scale[i]
        for c in range(2):
            at = (2 * i + c) * count
            out_ref[c, i, 0] = num[at : at + count] * both


def coherences(got, date_group, ref_blocks, look_offsets, days, looks, row_base):
    dates = date_group.shape[0] * days
    smem = pl.BlockSpec(memory_space=pltpu.SMEM)
    vmem = pl.BlockSpec(memory_space=pltpu.VMEM)
    return pl.pallas_call(
        functools.partial(look_kernel, days, row_base),
        out_shape=jax.ShapeDtypeStruct((2, looks, 1, NREF * REF_BLK, dates), jnp.float32),
        in_specs=[smem, smem, smem, vmem],
        out_specs=vmem,
        compiler_params=pltpu.CompilerParams(vmem_limit_bytes=24 * 1024 * 1024),
    )(date_group, ref_blocks, look_offsets, got)


def body(slc, date_group, ref_blocks, look_offsets):
    days, rows = slc.shape[1:3]
    n_date, n_pol = lax.axis_size("date"), lax.axis_size("pol")
    looks = rows // STRIDE // n_pol
    assert slc.shape[3] == n_date * STRIDE
    if lax.axis_size("tile") == 1 and n_pol == 1:
        x, row_base = slc[None], 0
    else:
        rimmed = with_halo(slc, "tile", 2, RIM)
        step = looks * STRIDE
        x = jnp.stack([rimmed[:, :, p * step : (p + 1) * step + 2 * RIM] for p in range(n_pol)])
        row_base = -RIM
    got = exchange(x, n_date, n_pol)
    if days % 8:
        got = jnp.transpose(got, (1, 0, 2, 3)).reshape(SPAN, n_date * n_pol * days, -1)
    return coherences(got, date_group, ref_blocks, look_offsets, days, looks, row_base)


def solution(mesh):
    return jax.shard_map(
        body,
        mesh=mesh,
        in_specs=(P(None, ("date", "pol"), ("groups", "tile"), None), P(), P(), P()),
        out_specs=P(None, ("groups", "tile", "pol"), "date", None, None),
        check_vma=False,
    )
```

```python
import functools
import math

import jax
import jax.numpy as jnp
from jax import lax
from jax.experimental import pallas as pl
from jax.experimental.pallas import tpu as pltpu
from jax.sharding import PartitionSpec as P

REF_BLK = 16
NREF = 4
STRIDE = 4
WIN = 9
RIM = WIN // 2
PLANE = 8
SPAN = 3


def with_halo(cells, axis, dim, width):
    count = lax.axis_size(axis)
    ends = count - 1
    head = lax.slice_in_dim(cells, 0, width, axis=dim)
    tail = lax.slice_in_dim(cells, cells.shape[dim] - width, cells.shape[dim], axis=dim)
    return jnp.concatenate(
        [
            lax.ppermute(tail, axis, [(i, i + 1) for i in range(ends)]),
            cells,
            lax.ppermute(head, axis, [(i + 1, i) for i in range(ends)]),
        ],
        axis=dim,
    )


def nt_dot(a, b):
    return lax.dot_general(
        a, b, (((1,), (1,)), ((), ())), preferred_element_type=jnp.float32
    )


def iota(shape, dim):
    return lax.broadcasted_iota(jnp.int32, shape, dim)


def pack(x_ref, p, col_blocks):
    _, _, days, rows, cols = x_ref.shape
    lanes = 2 * rows * STRIDE
    tall = jnp.concatenate(
        [jnp.concatenate([x_ref[p, 0, d], x_ref[p, 1, d]], axis=0) for d in range(days)], axis=1
    )
    spread = (iota((lanes, 2 * rows), 0) // STRIDE == iota((lanes, 2 * rows), 1))
    wide = jnp.dot(spread.astype(jnp.bfloat16), tall, preferred_element_type=jnp.float32)
    keep = iota(wide.shape, 0) % STRIDE == iota(wide.shape, 1) % STRIDE
    wide = jnp.where(keep, wide, 0.0).astype(jnp.bfloat16)
    shape = (col_blocks * days, days * cols)
    row_id, lane_id = iota(shape, 0), iota(shape, 1)
    pick = (row_id // days == (lane_id % cols) // STRIDE) & (row_id % days == lane_id // cols)
    pick = jnp.where(pick, 1.0, 0.0).astype(jnp.bfloat16)
    return nt_dot(pick, wide).reshape(col_blocks, days, lanes)


def flipped(number, bits):
    bit = 1
    while bit <= bits:
        if bits & bit:
            number = number + bit - 2 * bit * lax.rem(number // bit, 2)
        bit *= 2
    return number


def exchange_kernel(
    n_plane, side, n_pol, x_ref, got_ref, blocks, stage, send_one, recv_one, send_two, recv_two
):
    n_date, first = n_plane * side, n_plane * n_pol
    my_date, my_pol = lax.axis_index("date"), lax.axis_index("pol")
    my_plane, my_place = my_date // side, lax.rem(my_date, side)
    me = my_plane * n_pol + my_pol

    def across(t):
        other = flipped(me, t)
        plane, pol = other // n_pol, lax.rem(other, n_pol)
        return other, plane, pol, {"date": plane * side + my_place, "pol": pol}

    def beside(k):
        place = lax.rem(my_place + k, side)
        return place, {"date": my_plane * side + place, "pol": my_pol}

    barrier = pltpu.get_barrier_semaphore()
    mesh_ids = pl.DeviceIdType.MESH

    def greet(k, carry):
        pl.semaphore_signal(barrier, inc=1, device_id=beside(k)[1], device_id_type=mesh_ids)
        return carry

    for t in range(first - 1, 0, -1):
        pl.semaphore_signal(barrier, inc=1, device_id=across(t)[3], device_id_type=mesh_ids)
    lax.fori_loop(1, side, greet, 0)

    zero = jnp.zeros((1,) + blocks.shape[2:], blocks.dtype)
    for p in range(n_pol):
        blocks[p, 0:1] = zero
        blocks[p, n_date + 1 : n_date + 2] = zero
        blocks[p, 1 : n_date + 1] = pack(x_ref, p, n_date).astype(blocks.dtype)

    pl.semaphore_wait(barrier, first + side - 2)

    reach = side + SPAN - 1
    for t in range(first - 1, 0, -1):
        _, plane, pol, device = across(t)
        pltpu.make_async_remote_copy(
            src_ref=blocks.at[pol, pl.ds(plane * side, reach)],
            dst_ref=stage.at[me],
            send_sem=send_one,
            recv_sem=recv_one.at[me],
            device_id=device,
            device_id_type=mesh_ids,
        ).start()

    def share(origin, source, start):
        def give(k, carry):
            place, device = beside(k)
            pltpu.make_async_remote_copy(
                src_ref=source.at[pl.ds(start + place, SPAN)],
                dst_ref=got_ref.at[origin, my_place],
                send_sem=send_two,
                recv_sem=recv_two,
                device_id=device,
                device_id_type=mesh_ids,
            ).start()
            return carry

        lax.fori_loop(1, side, give, 0)
        pltpu.make_async_copy(
            source.at[pl.ds(start + my_place, SPAN)], got_ref.at[origin, my_place], recv_two
        ).start()

    share(me, blocks.at[my_pol], my_plane * side)
    for t in range(1, first):
        other = across(t)[0]
        pltpu.make_async_copy(stage.at[other], stage.at[other], recv_one.at[other]).wait()
        share(other, stage.at[other], 0)

    pltpu.make_async_copy(got_ref, got_ref, recv_two).wait()
    sent = stage.at[pl.ds(0, first - 1)]
    pltpu.make_async_copy(sent, sent, send_one).wait()
    sent = got_ref.at[:, pl.ds(0, side - 1)]
    pltpu.make_async_copy(sent, sent, send_two).wait()


def exchange(x, n_date, n_pol):
    _, _, days, rows, _ = x.shape
    lanes = 2 * rows * STRIDE
    side = math.gcd(n_date, PLANE)
    n_plane = n_date // side
    first = n_plane * n_pol
    got = pl.pallas_call(
        functools.partial(exchange_kernel, n_plane, side, n_pol),
        out_shape=jax.ShapeDtypeStruct((first, side, SPAN, days, lanes), x.dtype),
        in_specs=[pl.BlockSpec(memory_space=pltpu.VMEM)],
        out_specs=pl.BlockSpec(memory_space=pltpu.VMEM),
        scratch_shapes=[
            pltpu.VMEM((n_pol, n_date + SPAN - 1, days, lanes), x.dtype),
            pltpu.VMEM((first, side + SPAN - 1, days, lanes), x.dtype),
            pltpu.SemaphoreType.DMA,
            pltpu.SemaphoreType.DMA((first,)),
            pltpu.SemaphoreType.DMA,
            pltpu.SemaphoreType.DMA,
        ],
        compiler_params=pltpu.CompilerParams(
            collective_id=0, has_side_effects=True, vmem_limit_bytes=24 * 1024 * 1024
        ),
    )(x)
    if n_pol > 1:
        got = got.reshape(n_plane, n_pol, side, SPAN, days, lanes)
        got = jnp.swapaxes(got, 1, 2)
    return got.reshape(n_date * n_pol, SPAN, days, lanes)


def look_kernel(days, row_base, group_ref, refs_ref, offs_ref, got_ref, out_ref):
    sources = group_ref.shape[0]
    dates = sources * days
    if got_ref.shape[0] == SPAN:
        stored = [got_ref[m] for m in range(SPAN)]
    else:
        stored = [
            got_ref[:, m].astype(jnp.float32).reshape(dates, got_ref.shape[-1]).astype(jnp.bfloat16)
            for m in range(SPAN)
        ]
    lanes = stored[0].shape[1]
    stored = jnp.concatenate(stored, axis=1)
    width = SPAN * lanes

    slot = iota((1, dates), 1)
    held = jnp.zeros((1, dates), jnp.int32)
    for s in range(sources):
        held = jnp.where(slot // days == s, group_ref[s], held)
    held = held * days + slot % days
    ref_id = iota((NREF * REF_BLK, 1), 0)
    wanted = jnp.zeros(ref_id.shape, jnp.int32)
    for b in range(NREF):
        wanted = jnp.where(ref_id // REF_BLK == b, refs_ref[b], wanted)
    wanted = wanted * REF_BLK + ref_id % REF_BLK
    order = jnp.where(iota((dates, dates), 0) == held, 1.0, 0.0).astype(jnp.bfloat16)
    ref_order = jnp.where(wanted == held, 1.0, 0.0).astype(jnp.bfloat16)
    vals = jnp.dot(order, stored, preferred_element_type=jnp.float32)
    refs = jnp.dot(ref_order, stored, preferred_element_type=jnp.float32)

    half = lanes // 2
    turned = jnp.concatenate(
        [pltpu.roll(refs[:, m * lanes : (m + 1) * lanes], half, 1) for m in range(SPAN)], axis=1
    )
    turned = jnp.where(iota(turned.shape, 1) % lanes < half, -turned, turned)

    def window(rows, look):
        lane = iota((rows, width), 1)
        col = (lane // lanes - 1) * STRIDE + lane % STRIDE - offs_ref[1]
        row = (lane % half) // STRIDE + row_base - STRIDE * look - offs_ref[0]
        return (jnp.abs(col) <= RIM) & (jnp.abs(row) <= RIM)

    looks = out_ref.shape[1]
    square = vals * vals
    high = square.astype(jnp.bfloat16)
    low = (square - high.astype(jnp.float32)).astype(jnp.bfloat16)
    boxes = jnp.where(window(8, iota((8, width), 0)), 1.0, 0.0).astype(jnp.bfloat16)
    scale = lax.rsqrt(nt_dot(boxes, high) + nt_dot(boxes, low))

    parts, ref_scale = [], []
    for i in range(looks):
        box = jnp.where(window(1, i), 1.0, 0.0)
        here = refs * box
        parts += [here.astype(jnp.bfloat16), (turned * box).astype(jnp.bfloat16)]
        ref_scale.append(lax.rsqrt(jnp.sum(here * here, axis=1, keepdims=True)))
    num = nt_dot(jnp.concatenate(parts, axis=0), vals.astype(jnp.bfloat16))
    count = NREF * REF_BLK
    for i in range(looks):
        both = scale[i : i + 1] * ref_scale[i]
        for c in range(2):
            at = (2 * i + c) * count
            out_ref[c, i, 0] = num[at : at + count] * both


def coherences(got, date_group, ref_blocks, look_offsets, days, looks, row_base):
    dates = date_group.shape[0] * days
    smem = pl.BlockSpec(memory_space=pltpu.SMEM)
    vmem = pl.BlockSpec(memory_space=pltpu.VMEM)
    return pl.pallas_call(
        functools.partial(look_kernel, days, row_base),
        out_shape=jax.ShapeDtypeStruct((2, looks, 1, NREF * REF_BLK, dates), jnp.float32),
        in_specs=[smem, smem, smem, vmem],
        out_specs=vmem,
        compiler_params=pltpu.CompilerParams(vmem_limit_bytes=24 * 1024 * 1024),
    )(date_group, ref_blocks, look_offsets, got)


def body(slc, date_group, ref_blocks, look_offsets):
    days, rows = slc.shape[1:3]
    n_date, n_pol = lax.axis_size("date"), lax.axis_size("pol")
    looks = rows // STRIDE // n_pol
    assert slc.shape[3] == n_date * STRIDE
    if lax.axis_size("tile") == 1 and n_pol == 1:
        x, row_base = slc[None], 0
    else:
        rimmed = with_halo(slc, "tile", 2, RIM)
        step = looks * STRIDE
        x = jnp.stack([rimmed[:, :, p * step : (p + 1) * step + 2 * RIM] for p in range(n_pol)])
        row_base = -RIM
    got = exchange(x, n_date, n_pol)
    if days % 8:
        got = jnp.transpose(got, (1, 0, 2, 3)).reshape(SPAN, n_date * n_pol * days, -1)
    return coherences(got, date_group, ref_blocks, look_offsets, days, looks, row_base)


def solution(mesh):
    return jax.shard_map(
        body,
        mesh=mesh,
        in_specs=(P(None, ("date", "pol"), ("groups", "tile"), None), P(), P(), P()),
        out_specs=P(None, ("groups", "tile", "pol"), "date", None, None),
        check_vma=False,
    )
```

```python
import functools

import jax
import jax.numpy as jnp
from jax import lax
from jax.experimental import pallas as pl
from jax.experimental.pallas import tpu as pltpu
from jax.sharding import PartitionSpec as P

REF_BLK = 16
NREF = 4
STRIDE = 4
WIN = 9
RIM = WIN // 2
SPAN = 3


def with_halo(cells, axis, dim, width):
    count = lax.axis_size(axis)
    ends = count - 1
    head = lax.slice_in_dim(cells, 0, width, axis=dim)
    tail = lax.slice_in_dim(cells, cells.shape[dim] - width, cells.shape[dim], axis=dim)
    return jnp.concatenate(
        [
            lax.ppermute(tail, axis, [(i, i + 1) for i in range(ends)]),
            cells,
            lax.ppermute(head, axis, [(i + 1, i) for i in range(ends)]),
        ],
        axis=dim,
    )


def nt_dot(a, b):
    return lax.dot_general(
        a, b, (((1,), (1,)), ((), ())), preferred_element_type=jnp.float32
    )


def iota(shape, dim):
    return lax.broadcasted_iota(jnp.int32, shape, dim)


def over(ids, size):
    if size & (size - 1):
        return ids // size
    return ids >> (size.bit_length() - 1)


def within(ids, size):
    if size & (size - 1):
        return ids % size
    return ids & (size - 1)


def pack(x_ref, p, col_blocks):
    _, _, days, rows, cols = x_ref.shape
    lanes = 2 * rows * STRIDE
    tall = jnp.concatenate(
        [jnp.concatenate([x_ref[p, 0, d], x_ref[p, 1, d]], axis=0) for d in range(days)], axis=1
    )
    spread = over(iota((lanes, 2 * rows), 0), STRIDE) == iota((lanes, 2 * rows), 1)
    spread = jnp.where(spread, 1.0, 0.0).astype(jnp.bfloat16)
    wide = jnp.dot(spread, tall, preferred_element_type=jnp.float32)
    lane = iota((1, days * cols), 1)
    keep = within(iota((lanes, 1), 0), STRIDE) == within(lane, STRIDE)
    wide = jnp.where(keep, wide, 0.0).astype(jnp.bfloat16)
    target = over(within(lane, cols), STRIDE) * days + over(lane, cols)
    pick = iota((col_blocks * days, days * cols), 0) == target
    pick = jnp.where(pick, 1.0, 0.0).astype(jnp.bfloat16)
    return nt_dot(pick, wide).reshape(col_blocks, days, lanes)


def exchange_kernel(n_date, n_pol, x_ref, got_ref, blocks, send_sem, recv_sem):
    n = n_date * n_pol
    my_date, my_pol = lax.axis_index("date"), lax.axis_index("pol")
    me = my_date * n_pol + my_pol

    def place(k):
        other = lax.rem(me + k, n)
        if n_pol == 1:
            return other, 0
        return other // n_pol, lax.rem(other, n_pol)

    barrier = pltpu.get_barrier_semaphore()

    def greet(k, carry):
        date, pol = place(k)
        pl.semaphore_signal(
            barrier,
            inc=1,
            device_id={"date": date, "pol": pol},
            device_id_type=pl.DeviceIdType.MESH,
        )
        return carry

    lax.fori_loop(1, n, greet, 0)

    zero = jnp.zeros((1,) + blocks.shape[2:], blocks.dtype)
    for p in range(n_pol):
        blocks[p, 0:1] = zero
        blocks[p, n_date + 1 : n_date + 2] = zero
        blocks[p, 1 : n_date + 1] = pack(x_ref, p, n_date).astype(blocks.dtype)

    pl.semaphore_wait(barrier, n - 1)

    def send(k, carry):
        date, pol = place(k)
        pltpu.make_async_remote_copy(
            src_ref=blocks.at[pol, pl.ds(date, SPAN)],
            dst_ref=got_ref.at[me],
            send_sem=send_sem,
            recv_sem=recv_sem,
            device_id={"date": date, "pol": pol},
            device_id_type=pl.DeviceIdType.MESH,
        ).start()
        return carry

    lax.fori_loop(1, n, send, 0)
    pltpu.make_async_copy(
        blocks.at[my_pol, pl.ds(my_date, SPAN)], got_ref.at[me], recv_sem
    ).start()
    pltpu.make_async_copy(got_ref, got_ref, recv_sem).wait()
    sent = got_ref.at[pl.ds(0, n - 1)]
    pltpu.make_async_copy(sent, sent, send_sem).wait()


def exchange(x, n_date, n_pol):
    _, _, days, rows, _ = x.shape
    lanes = 2 * rows * STRIDE
    n = n_date * n_pol
    return pl.pallas_call(
        functools.partial(exchange_kernel, n_date, n_pol),
        out_shape=jax.ShapeDtypeStruct((n, SPAN, days, lanes), x.dtype),
        in_specs=[pl.BlockSpec(memory_space=pltpu.VMEM)],
        out_specs=pl.BlockSpec(memory_space=pltpu.VMEM),
        scratch_shapes=[
            pltpu.VMEM((n_pol, n_date + SPAN - 1, days, lanes), x.dtype),
            pltpu.SemaphoreType.DMA,
            pltpu.SemaphoreType.DMA,
        ],
        compiler_params=pltpu.CompilerParams(
            collective_id=0, has_side_effects=True, vmem_limit_bytes=24 * 1024 * 1024
        ),
    )(x)


def look_kernel(days, row_base, group_ref, refs_ref, offs_ref, got_ref, out_ref):
    sources = group_ref.shape[0]
    dates = sources * days
    if got_ref.shape[0] == SPAN:
        stored = [got_ref[m] for m in range(SPAN)]
    else:
        stored = [
            got_ref[:, m].astype(jnp.float32).reshape(dates, got_ref.shape[-1]).astype(jnp.bfloat16)
            for m in range(SPAN)
        ]
    lanes = stored[0].shape[1]
    stored = jnp.concatenate(stored, axis=1)
    width = SPAN * lanes

    slot = iota((1, dates), 1)
    held = jnp.zeros((1, dates), jnp.int32)
    block = over(slot, days)
    for s in range(sources):
        held = jnp.where(block == s, group_ref[s], held)
    held = held * days + within(slot, days)
    ref_id = iota((NREF * REF_BLK, 1), 0)
    wanted = jnp.zeros(ref_id.shape, jnp.int32)
    for b in range(NREF):
        wanted = jnp.where(over(ref_id, REF_BLK) == b, refs_ref[b], wanted)
    wanted = wanted * REF_BLK + within(ref_id, REF_BLK)
    order = jnp.where(iota((dates, dates), 0) == held, 1.0, 0.0).astype(jnp.bfloat16)
    ref_order = jnp.where(wanted == held, 1.0, 0.0).astype(jnp.bfloat16)
    vals = jnp.dot(order, stored, preferred_element_type=jnp.float32)
    refs = jnp.dot(ref_order, stored, preferred_element_type=jnp.float32)

    half = lanes // 2
    turned = jnp.concatenate(
        [pltpu.roll(refs[:, m * lanes : (m + 1) * lanes], half, 1) for m in range(SPAN)], axis=1
    )
    sign = jnp.where(within(iota((1, width), 1), lanes) < half, -1.0, 1.0)
    turned = turned * sign

    def window(rows, look):
        lane = iota((rows, width), 1)
        col = (over(lane, lanes) - 1) * STRIDE + within(lane, STRIDE) - offs_ref[1]
        row = over(within(lane, half), STRIDE) + row_base - STRIDE * look - offs_ref[0]
        return (jnp.abs(col) <= RIM) & (jnp.abs(row) <= RIM)

    looks = out_ref.shape[1]
    square = vals * vals
    high = square.astype(jnp.bfloat16)
    low = (square - high.astype(jnp.float32)).astype(jnp.bfloat16)
    boxes = jnp.where(window(8, iota((8, width), 0)), 1.0, 0.0).astype(jnp.bfloat16)
    scale = lax.rsqrt(nt_dot(boxes, high) + nt_dot(boxes, low))

    parts, ref_scale = [], []
    for i in range(looks):
        box = jnp.where(window(1, i), 1.0, 0.0)
        here = refs * box
        parts += [here.astype(jnp.bfloat16), (turned * box).astype(jnp.bfloat16)]
        ref_scale.append(lax.rsqrt(jnp.sum(here * here, axis=1, keepdims=True)))
    num = nt_dot(jnp.concatenate(parts, axis=0), vals.astype(jnp.bfloat16))
    count = NREF * REF_BLK
    for i in range(looks):
        both = scale[i : i + 1] * ref_scale[i]
        for c in range(2):
            at = (2 * i + c) * count
            out_ref[c, i, 0] = num[at : at + count] * both


def coherences(got, date_group, ref_blocks, look_offsets, days, looks, row_base):
    dates = date_group.shape[0] * days
    smem = pl.BlockSpec(memory_space=pltpu.SMEM)
    vmem = pl.BlockSpec(memory_space=pltpu.VMEM)
    return pl.pallas_call(
        functools.partial(look_kernel, days, row_base),
        out_shape=jax.ShapeDtypeStruct((2, looks, 1, NREF * REF_BLK, dates), jnp.float32),
        in_specs=[smem, smem, smem, vmem],
        out_specs=vmem,
        compiler_params=pltpu.CompilerParams(vmem_limit_bytes=24 * 1024 * 1024),
    )(date_group, ref_blocks, look_offsets, got)


def body(slc, date_group, ref_blocks, look_offsets):
    days, rows = slc.shape[1:3]
    n_date, n_pol = lax.axis_size("date"), lax.axis_size("pol")
    looks = rows // STRIDE // n_pol
    assert slc.shape[3] == n_date * STRIDE
    if lax.axis_size("tile") == 1 and n_pol == 1:
        x, row_base = slc[None], 0
    else:
        rimmed = with_halo(slc, "tile", 2, RIM)
        step = looks * STRIDE
        x = jnp.stack([rimmed[:, :, p * step : (p + 1) * step + 2 * RIM] for p in range(n_pol)])
        row_base = -RIM
    got = exchange(x, n_date, n_pol)
    if days % 8:
        got = jnp.transpose(got, (1, 0, 2, 3)).reshape(SPAN, n_date * n_pol * days, -1)
    return coherences(got, date_group, ref_blocks, look_offsets, days, looks, row_base)


def solution(mesh):
    return jax.shard_map(
        body,
        mesh=mesh,
        in_specs=(P(None, ("date", "pol"), ("groups", "tile"), None), P(), P(), P()),
        out_specs=P(None, ("groups", "tile", "pol"), "date", None, None),
        check_vma=False,
    )
```

```python
import functools

import jax
import jax.numpy as jnp
from jax import lax
from jax.experimental import pallas as pl
from jax.experimental.pallas import tpu as pltpu
from jax.sharding import PartitionSpec as P

REF_BLK = 16
NREF = 4
STRIDE = 4
WIN = 9
RIM = WIN // 2
SPAN = 3


def with_halo(cells, axis, dim, width):
    count = lax.axis_size(axis)
    ends = count - 1
    head = lax.slice_in_dim(cells, 0, width, axis=dim)
    tail = lax.slice_in_dim(cells, cells.shape[dim] - width, cells.shape[dim], axis=dim)
    return jnp.concatenate(
        [
            lax.ppermute(tail, axis, [(i, i + 1) for i in range(ends)]),
            cells,
            lax.ppermute(head, axis, [(i + 1, i) for i in range(ends)]),
        ],
        axis=dim,
    )


def nt_dot(a, b):
    return lax.dot_general(
        a, b, (((1,), (1,)), ((), ())), preferred_element_type=jnp.float32
    )


def iota(shape, dim):
    return lax.broadcasted_iota(jnp.int32, shape, dim)


def over(ids, size):
    if size & (size - 1):
        return ids // size
    return ids >> (size.bit_length() - 1)


def within(ids, size):
    if size & (size - 1):
        return ids % size
    return ids & (size - 1)


def pack(x_ref, p, col_blocks):
    _, _, days, rows, cols = x_ref.shape
    lanes = 2 * rows * STRIDE
    tall = jnp.concatenate(
        [jnp.concatenate([x_ref[p, 0, d], x_ref[p, 1, d]], axis=0) for d in range(days)], axis=1
    )
    spread = over(iota((lanes, 2 * rows), 0), STRIDE) == iota((lanes, 2 * rows), 1)
    spread = jnp.where(spread, 1.0, 0.0).astype(jnp.bfloat16)
    wide = jnp.dot(spread, tall, preferred_element_type=jnp.float32)
    lane = iota((1, days * cols), 1)
    keep = within(iota((lanes, 1), 0), STRIDE) == within(lane, STRIDE)
    wide = jnp.where(keep, wide, 0.0).astype(jnp.bfloat16)
    target = over(within(lane, cols), STRIDE) * days + over(lane, cols)
    pick = iota((col_blocks * days, days * cols), 0) == target
    pick = jnp.where(pick, 1.0, 0.0).astype(jnp.bfloat16)
    return nt_dot(pick, wide).reshape(col_blocks, days, lanes)


def exchange_kernel(n_date, n_pol, x_ref, got_ref, blocks, send_sem, recv_sem):
    n = n_date * n_pol
    my_date, my_pol = lax.axis_index("date"), lax.axis_index("pol")
    me = my_date * n_pol + my_pol

    def place(k):
        other = lax.rem(me + k, n)
        if n_pol == 1:
            return other, 0
        return other // n_pol, lax.rem(other, n_pol)

    barrier = pltpu.get_barrier_semaphore()

    def greet(k, carry):
        date, pol = place(k)
        pl.semaphore_signal(
            barrier,
            inc=1,
            device_id={"date": date, "pol": pol},
            device_id_type=pl.DeviceIdType.MESH,
        )
        return carry

    lax.fori_loop(1, n, greet, 0)

    zero = jnp.zeros((1,) + blocks.shape[2:], blocks.dtype)
    for p in range(n_pol):
        blocks[p, 0:1] = zero
        blocks[p, n_date + 1 : n_date + 2] = zero
        blocks[p, 1 : n_date + 1] = pack(x_ref, p, n_date).astype(blocks.dtype)

    pl.semaphore_wait(barrier, n - 1)

    def send(step, carry):
        date, pol = place(n // 2 + (step // 2) * (2 * lax.rem(step, 2) - 1))
        pltpu.make_async_remote_copy(
            src_ref=blocks.at[pol, pl.ds(date, SPAN)],
            dst_ref=got_ref.at[me],
            send_sem=send_sem,
            recv_sem=recv_sem,
            device_id={"date": date, "pol": pol},
            device_id_type=pl.DeviceIdType.MESH,
        ).start()
        return carry

    lax.fori_loop(1, n, send, 0)
    pltpu.make_async_copy(
        blocks.at[my_pol, pl.ds(my_date, SPAN)], got_ref.at[me], recv_sem
    ).start()
    pltpu.make_async_copy(got_ref, got_ref, recv_sem).wait()
    sent = got_ref.at[pl.ds(0, n - 1)]
    pltpu.make_async_copy(sent, sent, send_sem).wait()


def exchange(x, n_date, n_pol):
    _, _, days, rows, _ = x.shape
    lanes = 2 * rows * STRIDE
    n = n_date * n_pol
    return pl.pallas_call(
        functools.partial(exchange_kernel, n_date, n_pol),
        out_shape=jax.ShapeDtypeStruct((n, SPAN, days, lanes), x.dtype),
        in_specs=[pl.BlockSpec(memory_space=pltpu.VMEM)],
        out_specs=pl.BlockSpec(memory_space=pltpu.VMEM),
        scratch_shapes=[
            pltpu.VMEM((n_pol, n_date + SPAN - 1, days, lanes), x.dtype),
            pltpu.SemaphoreType.DMA,
            pltpu.SemaphoreType.DMA,
        ],
        compiler_params=pltpu.CompilerParams(
            collective_id=0, has_side_effects=True, vmem_limit_bytes=24 * 1024 * 1024
        ),
    )(x)


def look_kernel(days, row_base, group_ref, refs_ref, offs_ref, got_ref, out_ref):
    sources = group_ref.shape[0]
    dates = sources * days
    if got_ref.shape[0] == SPAN:
        stored = [got_ref[m] for m in range(SPAN)]
    else:
        stored = [
            got_ref[:, m].astype(jnp.float32).reshape(dates, got_ref.shape[-1]).astype(jnp.bfloat16)
            for m in range(SPAN)
        ]
    lanes = stored[0].shape[1]
    stored = jnp.concatenate(stored, axis=1)
    width = SPAN * lanes

    slot = iota((1, dates), 1)
    held = jnp.zeros((1, dates), jnp.int32)
    block = over(slot, days)
    for s in range(sources):
        held = jnp.where(block == s, group_ref[s], held)
    held = held * days + within(slot, days)
    ref_id = iota((NREF * REF_BLK, 1), 0)
    wanted = jnp.zeros(ref_id.shape, jnp.int32)
    for b in range(NREF):
        wanted = jnp.where(over(ref_id, REF_BLK) == b, refs_ref[b], wanted)
    wanted = wanted * REF_BLK + within(ref_id, REF_BLK)
    order = jnp.where(iota((dates, dates), 0) == held, 1.0, 0.0).astype(jnp.bfloat16)
    ref_order = jnp.where(wanted == held, 1.0, 0.0).astype(jnp.bfloat16)
    vals = jnp.dot(order, stored, preferred_element_type=jnp.float32)
    refs = jnp.dot(ref_order, stored, preferred_element_type=jnp.float32)

    half = lanes // 2
    turned = jnp.concatenate(
        [pltpu.roll(refs[:, m * lanes : (m + 1) * lanes], half, 1) for m in range(SPAN)], axis=1
    )
    sign = jnp.where(within(iota((1, width), 1), lanes) < half, -1.0, 1.0)
    turned = turned * sign

    def window(rows, look):
        lane = iota((rows, width), 1)
        col = (over(lane, lanes) - 1) * STRIDE + within(lane, STRIDE) - offs_ref[1]
        row = over(within(lane, half), STRIDE) + row_base - STRIDE * look - offs_ref[0]
        return (jnp.abs(col) <= RIM) & (jnp.abs(row) <= RIM)

    looks = out_ref.shape[1]
    square = vals * vals
    high = square.astype(jnp.bfloat16)
    low = (square - high.astype(jnp.float32)).astype(jnp.bfloat16)
    boxes = jnp.where(window(8, iota((8, width), 0)), 1.0, 0.0).astype(jnp.bfloat16)
    scale = lax.rsqrt(nt_dot(boxes, high) + nt_dot(boxes, low))

    parts, ref_scale = [], []
    for i in range(looks):
        box = jnp.where(window(1, i), 1.0, 0.0)
        here = refs * box
        parts += [here.astype(jnp.bfloat16), (turned * box).astype(jnp.bfloat16)]
        ref_scale.append(lax.rsqrt(jnp.sum(here * here, axis=1, keepdims=True)))
    num = nt_dot(jnp.concatenate(parts, axis=0), vals.astype(jnp.bfloat16))
    count = NREF * REF_BLK
    for i in range(looks):
        both = scale[i : i + 1] * ref_scale[i]
        for c in range(2):
            at = (2 * i + c) * count
            out_ref[c, i, 0] = num[at : at + count] * both


def coherences(got, date_group, ref_blocks, look_offsets, days, looks, row_base):
    dates = date_group.shape[0] * days
    smem = pl.BlockSpec(memory_space=pltpu.SMEM)
    vmem = pl.BlockSpec(memory_space=pltpu.VMEM)
    return pl.pallas_call(
        functools.partial(look_kernel, days, row_base),
        out_shape=jax.ShapeDtypeStruct((2, looks, 1, NREF * REF_BLK, dates), jnp.float32),
        in_specs=[smem, smem, smem, vmem],
        out_specs=vmem,
        compiler_params=pltpu.CompilerParams(vmem_limit_bytes=24 * 1024 * 1024),
    )(date_group, ref_blocks, look_offsets, got)


def body(slc, date_group, ref_blocks, look_offsets):
    days, rows = slc.shape[1:3]
    n_date, n_pol = lax.axis_size("date"), lax.axis_size("pol")
    looks = rows // STRIDE // n_pol
    assert slc.shape[3] == n_date * STRIDE
    if lax.axis_size("tile") == 1 and n_pol == 1:
        x, row_base = slc[None], 0
    else:
        rimmed = with_halo(slc, "tile", 2, RIM)
        step = looks * STRIDE
        x = jnp.stack([rimmed[:, :, p * step : (p + 1) * step + 2 * RIM] for p in range(n_pol)])
        row_base = -RIM
    got = exchange(x, n_date, n_pol)
    if days % 8:
        got = jnp.transpose(got, (1, 0, 2, 3)).reshape(SPAN, n_date * n_pol * days, -1)
    return coherences(got, date_group, ref_blocks, look_offsets, days, looks, row_base)


def solution(mesh):
    return jax.shard_map(
        body,
        mesh=mesh,
        in_specs=(P(None, ("date", "pol"), ("groups", "tile"), None), P(), P(), P()),
        out_specs=P(None, ("groups", "tile", "pol"), "date", None, None),
        check_vma=False,
    )
```
